32 devices in a mesh: dp: 8 (over y, x, core), tensor: 4 (over z).
Axes of the slice: x: 2, y: 2, z: 4, core: 2. Of those that a mesh axis runs over, the one named last changes fastest.
Arguments:
- tokens: bfloat16 [32, 2048, 768], P('dp', 'tensor'), may hold values from -6 to 6
- segment_ids: int32 [32, 2048], P('dp'), may hold values from 0 to 4, as said below
- selected: int32 [32, 256], P('dp'), may hold values from 0 to 2047, as said below
- w_router: bfloat16 [768], replicated, may hold values from -0.21875 to 0.21875
- gain_one: float32 [768], replicated, may hold values from 0.5 to 1.5
- w_query: bfloat16 [768, 768], P(None, 'tensor'), may hold values from -0.21875 to 0.21875
- w_key: bfloat16 [768, 768], P(None, 'tensor'), may hold values from -0.21875 to 0.21875
- w_value: bfloat16 [768, 768], P(None, 'tensor'), may hold values from -0.21875 to 0.21875
- w_out: bfloat16 [768, 768], P('tensor'), may hold values from -0.75 to 0.75
- gain_two: float32 [768], replicated, may hold values from 0.5 to 1.5
- w_up: bfloat16 [768, 3072], P(None, 'tensor'), may hold values from -0.21875 to 0.21875
- w_down: bfloat16 [3072, 768], P('tensor'), may hold values from -0.109375 to 0.109375
- grad_out: bfloat16 [32, 2048, 768], P('dp', 'tensor'), may hold values from -6 to 6
Outputs:
- layer_out: bfloat16 [32, 2048, 768], P('dp', 'tensor')
- grad_tokens: bfloat16 [32, 2048, 768], P('dp', 'tensor')
- grad_router: float32 [768], replicated
- grad_gain_one: float32 [768], replicated
- grad_query: float32 [768, 768], P(None, 'tensor')
- grad_key: float32 [768, 768], P(None, 'tensor')
- grad_value: float32 [768, 768], P(None, 'tensor')
- grad_out_proj: float32 [768, 768], P('tensor')
- grad_gain_two: float32 [768], replicated
- grad_up: float32 [768, 3072], P(None, 'tensor')
- grad_down: float32 [3072, 768], P('tensor')
The draws below stay inside these ranges and needn't reach their ends.
Inputs may be any that keep to these rules, and one draw needn't show every extreme that they name: `selected`: in each row the 256 positions are distinct and increasing, and every row names position 0 and position 2047. `segment_ids`: document numbers never fall along a row; each row starts with document 0 and ends with document 4.
All inputs are finite; a program needn't handle non-finite values.
Results may differ from the reference program's by a relative error of at most 0.018.
Values may be sent and summed in bfloat16 or wider, within the bound.
No kernel may reach another device: no remote copies, remote signals or barrier semaphores. Data moves between devices by JAX's collectives and lax.ppermute only.
A program may use at most 128 MiB of HBM per device.

```python
import jax
import jax.numpy as jnp
from jax import lax

D = 768
HEADS = 12
HD = 64
FF = 3072
ROW_LEN = 2048
PICKS = 256
ROWS = 32


def draw_segment_ids(key, part):
    key = jax.random.fold_in(key, 11)
    keys_all = jax.random.split(key, ROWS)

    def one_row(row_key):
        parts_keys = jax.random.split(row_key, 4)
        first_end = jax.random.randint(parts_keys[0], (), 1, ROW_LEN // 8)
        long_end = ROW_LEN - jax.random.randint(parts_keys[1], (), 2, ROW_LEN // 8)
        cut_one = jax.random.randint(parts_keys[2], (), long_end + 1, ROW_LEN)
        cut_two = jax.random.randint(parts_keys[3], (), long_end + 1, ROW_LEN)
        position = jnp.arange(ROW_LEN, dtype=jnp.int32)
        return (position >= first_end).astype(jnp.int32) + (position >= long_end).astype(jnp.int32) + (position >= cut_one).astype(jnp.int32) + (position >= cut_two).astype(jnp.int32)
    return jax.vmap(one_row)(keys_all)


def draw_selected(key, part):
    key = jax.random.fold_in(key, 23)
    keys_all = jax.random.split(key, ROWS)

    def one_row(row_key):
        inner = jax.random.permutation(row_key, ROW_LEN - 2)[:PICKS - 2].astype(jnp.int32) + 1
        ends = jnp.array([0, ROW_LEN - 1], dtype=jnp.int32)
        return jnp.sort(jnp.concatenate([ends, inner]))
    return jax.vmap(one_row)(keys_all)


def block_levels(rng, dims, pieces, least, top_value):
    level = 1.0
    for dim, shards_of in pieces:
        steps = jax.random.uniform(jax.random.fold_in(jax.random.fold_in(rng, 6), dim), (shards_of,), jnp.float32, least / len(pieces), top_value / len(pieces))
        level = level * jnp.repeat(jnp.exp(steps), dims[dim] // shards_of).reshape((-1,) + (1,) * (len(dims) - 1 - dim))
    return level


def bell_draw(stream_key, shape, deviation, limit, cuts=(), kind=jnp.bfloat16):
    values = deviation * jax.random.normal(stream_key, shape, jnp.float32)
    if cuts:
        values = values * block_levels(stream_key, shape, cuts, -0.22, 0.18)
    return jnp.clip(values, -limit, limit).astype(kind)


def setup_inputs(seed: int = 0) -> dict:
    arg_keys = jax.random.split(jax.random.key(seed), 14)
    return {
        "tokens": bell_draw(arg_keys[0], (ROWS, ROW_LEN, D), 1.0, 6.0, ((0, 8), (1, 4))),
        "segment_ids": draw_segment_ids(jax.random.fold_in(arg_keys[13], 71), 0),
        "selected": draw_selected(jax.random.fold_in(arg_keys[13], 71), 0),
        "w_router": bell_draw(arg_keys[3], (D,), D ** -0.5, 0.21875),
        "gain_one": jnp.clip(1.0 + 0.1 * jax.random.normal(arg_keys[4], (D,), jnp.float32), 0.5, 1.5),
        "w_query": bell_draw(arg_keys[5], (D, HEADS * HD), D ** -0.5, 0.21875, ((1, 4),)),
        "w_key": bell_draw(arg_keys[6], (D, HEADS * HD), D ** -0.5, 0.21875, ((1, 4),)),
        "w_value": bell_draw(arg_keys[7], (D, HEADS * HD), D ** -0.5, 0.21875, ((1, 4),)),
        "w_out": bell_draw(arg_keys[8], (HEADS * HD, D), HD ** -0.5, 0.75, ((0, 4),)),
        "gain_two": jnp.clip(1.0 + 0.1 * jax.random.normal(arg_keys[9], (D,), jnp.float32), 0.5, 1.5),
        "w_up": bell_draw(arg_keys[10], (D, FF), D ** -0.5, 0.21875, ((1, 4),)),
        "w_down": bell_draw(arg_keys[11], (FF, D), FF ** -0.5, 0.109375, ((0, 4),)),
        "grad_out": bell_draw(arg_keys[12], (ROWS, ROW_LEN, D), 1.0, 6.0, ((0, 8), (1, 4))),
    }


@jax.custom_vjp
def low(v):
    return lax.optimization_barrier(v.astype(jnp.bfloat16)).astype(jnp.float32)

@jax.custom_vjp
def low_back(v):
    return v

def low_keep(v):
    return (low(v), None)

def low_pass(kept, grad):
    return (grad,)

def back_keep(v):
    return (v, None)

def back_low(kept, grad):
    return (low(grad),)
low.defvjp(low_keep, low_pass)
low_back.defvjp(back_keep, back_low)
EPS = 1e-06
NEG = -1e+30

def rms_norm(values, gain):
    return values * lax.rsqrt(lax.optimization_barrier(jnp.mean(values * values, -1, keepdims=True)) + EPS) * gain

def matmul_hi(left, right):
    return jnp.dot(left, right, precision=lax.Precision.HIGHEST)

def row_layer(row_tokens, row_segments, row_picks, w_router, gain_one, w_query, w_key, w_value, w_out, gain_two, w_up, w_down):
    router = matmul_hi(row_tokens, w_router)
    chosen = row_tokens[row_picks]
    gate = router[row_picks]
    tags = row_segments[row_picks]
    position = jnp.arange(PICKS)
    allowed = (tags[:, None] == tags[None, :]) & (position[:, None] >= position[None, :])
    normed = low(rms_norm(chosen, gain_one))
    query_rows = low(low_back(matmul_hi(normed, w_query))).reshape(PICKS, HEADS, HD)
    key_rows = low(low_back(matmul_hi(normed, w_key))).reshape(PICKS, HEADS, HD)
    value_rows = low(low_back(matmul_hi(normed, w_value))).reshape(PICKS, HEADS, HD)
    scores = jnp.einsum('qhd,khd->hqk', query_rows, key_rows, precision=lax.Precision.HIGHEST) * HD ** (-0.5)
    scores = low_back(scores)
    scores = jnp.where(allowed[None], scores, NEG)
    prob_table = jax.nn.softmax(scores, axis=-1)
    mixed = jnp.einsum('hqk,khd->qhd', low(prob_table), value_rows, precision=lax.Precision.HIGHEST)
    mixed = low(low_back(mixed.reshape(PICKS, HEADS * HD)))
    attended = low_back(matmul_hi(mixed, w_out))
    middle = chosen + attended
    normed_two = low(rms_norm(middle, gain_two))
    hidden_pre = low_back(matmul_hi(normed_two, w_up))
    hidden = low(jax.nn.gelu(hidden_pre))
    branch = low_back(matmul_hi(hidden, w_down))
    updated = chosen + gate[:, None] * (attended + branch)
    return row_tokens.at[row_picks].set(updated)

def reference(tokens, segment_ids, selected, w_router, gain_one, w_query, w_key, w_value, w_out, gain_two, w_up, w_down, grad_out):

    def forward(tok, wr, g_one, wq, wk, wv, wo, g_two, wu, wd):
        mapped = jax.vmap(row_layer, in_axes=(0, 0, 0, None, None, None, None, None, None, None, None, None))
        return mapped(tok, segment_ids, selected, wr, g_one, wq, wk, wv, wo, g_two, wu, wd)
    inputs = (tokens.astype(jnp.float32), w_router.astype(jnp.float32), gain_one.astype(jnp.float32), w_query.astype(jnp.float32), w_key.astype(jnp.float32), w_value.astype(jnp.float32), w_out.astype(jnp.float32), gain_two.astype(jnp.float32), w_up.astype(jnp.float32), w_down.astype(jnp.float32))
    result, pull = jax.vjp(forward, *inputs)
    grads = pull(grad_out.astype(jnp.float32))
    return (result.astype(jnp.bfloat16), grads[0].astype(jnp.bfloat16), grads[1], grads[2], grads[3], grads[4], grads[5], grads[6], grads[7], grads[8], grads[9])
```

```python
import functools

import jax
import jax.numpy as jnp
from jax import lax
from jax.experimental import pallas as pl
from jax.experimental.pallas import tpu as pltpu
from jax.sharding import PartitionSpec as P


HD = 64
EPS = 1e-06
NEG = -1e30
EXTRA = 16
VMEM_LIMIT = 48 * 1024 * 1024
F32 = jnp.float32
BF16 = jnp.bfloat16


def nn(left, right):
    return lax.dot_general(left, right, (((1,), (0,)), ((), ())), preferred_element_type=F32)


def nt(left, right):
    return lax.dot_general(left, right, (((1,), (1,)), ((), ())), preferred_element_type=F32)


def tn(left, right):
    return lax.dot_general(left, right, (((0,), (0,)), ((), ())), preferred_element_type=F32)


def inv_rms(values):
    return lax.rsqrt(jnp.mean(values * values, -1, keepdims=True) + EPS)


def load_weights(core, own, other, table):
    pieces = len(own)
    tensor_size, types, heads, width, _ = own[0].shape
    for which, refs in ((core, own), (1 - core, other)):
        for c in range(pieces):
            for z in range(tensor_size):
                for t in range(types):
                    for h in range(heads):
                        start = (z * heads + h) * HD + c * width
                        table[2 * which + t, start : start + width, :] = refs[c][z, t, h]


def allowed_mask(tag_col, tag_row):
    count = tag_row.shape[1]
    query = lax.broadcasted_iota(jnp.int32, (count, count), 0)
    key = lax.broadcasted_iota(jnp.int32, (count, count), 1)
    return (tag_col == tag_row) & (query >= key)


def attend_kernel(pieces, core_ref, x_ref, tag_col, tag_row, gain_one, gain_two, router, *refs):
    own, other = refs[:pieces], refs[pieces : 2 * pieces]
    q_ref, k_ref, v_ref, mixed_ref, lse_ref, att_ref, normed_two_ref, gate_ref, table = refs[
        2 * pieces :
    ]
    load_weights(core_ref[0], own, other, table)
    x = x_ref[...].astype(F32)
    gate_ref[...] = jnp.sum(x * router[...], -1, keepdims=True)
    normed = (x * inv_rms(x) * gain_one[...]).astype(BF16)
    q_ref[...] = nt(normed, table[0]).astype(BF16)
    k_ref[...] = nt(normed, table[1]).astype(BF16)
    v_ref[...] = nt(normed, table[2]).astype(BF16)
    allowed = allowed_mask(tag_col[...], tag_row[...])
    heads = q_ref.shape[1] // HD
    for h in range(heads):
        part = slice(h * HD, (h + 1) * HD)
        scores = jnp.where(allowed, nt(q_ref[:, part], k_ref[:, part]) * HD**-0.5, NEG)
        top = jnp.max(scores, -1, keepdims=True)
        shifted = jnp.exp(scores - top)
        total = jnp.sum(shifted, -1, keepdims=True)
        probs = (shifted / total).astype(BF16)
        mixed_ref[:, part] = nn(probs, v_ref[:, part]).astype(BF16)
        lse_ref[:, h : h + 1] = top + jnp.log(total)
    attended = nn(mixed_ref[...], table[3])
    att_ref[...] = attended
    middle = x + attended
    normed_two_ref[...] = (middle * inv_rms(middle) * gain_two[...]).astype(BF16)


GELU_A = 0.7978845608028654
GELU_B = 0.044715


def hidden_kernel(pieces, first, last, n2_own, n2_oth, db_own, db_oth, *refs):
    weights = refs[:pieces]
    refs = refs[pieces:]
    if not first:
        dn_in, br_in = refs[:2]
        refs = refs[2:]
    grads = refs[:pieces]
    outs = refs[pieces:]
    count = n2_own.shape[0]
    n2 = jnp.concatenate([n2_own[...], n2_oth[...]], 0)
    db = jnp.concatenate([db_own[...], db_oth[...]], 0)
    d_normed, branch = None, None
    for i in range(pieces):
        tensor_size, _, width, model = weights[i].shape
        rows = tensor_size * width
        up = weights[i][:, 0].reshape(rows, model)
        down = weights[i][:, 1].reshape(rows, model)
        pre = nt(n2, up)
        inner = jnp.tanh(GELU_A * (pre + GELU_B * pre * pre * pre))
        hidden = (0.5 * pre * (1.0 + inner)).astype(BF16)
        slope = 0.5 * (1.0 + inner) + 0.5 * pre * (1.0 - inner * inner) * (
            GELU_A * (1.0 + 3.0 * GELU_B * pre * pre)
        )
        d_pre = (nt(db, down) * slope).astype(BF16)
        branch_part = nn(hidden, down)
        d_normed_part = nn(d_pre, up)
        branch = branch_part if branch is None else branch + branch_part
        d_normed = d_normed_part if d_normed is None else d_normed + d_normed_part
        grads[i][:, 0] = tn(d_pre, n2).astype(BF16).reshape(tensor_size, width, model)
        grads[i][:, 1] = tn(hidden, db).astype(BF16).reshape(tensor_size, width, model)
    if not first:
        d_normed = d_normed + dn_in[...]
        branch = branch + br_in[...]
    if last:
        dn_own, dn_send, br_own, br_send = outs
        dn_own[...] = d_normed[:count]
        dn_send[...] = d_normed[count:].astype(BF16)
        br_own[...] = branch[:count]
        br_send[...] = branch[count:].astype(BF16)
    else:
        dn_out, br_out = outs
        dn_out[...] = d_normed
        br_out[...] = branch


def back_kernel(
    pieces,
    core_ref,
    x_ref,
    cg_ref,
    gate_ref,
    att_ref,
    br_own,
    br_recv,
    dn_own,
    dn_recv,
    q_ref,
    k_ref,
    v_ref,
    mixed_ref,
    lse_ref,
    tag_col,
    tag_row,
    gain_one,
    gain_two,
    router,
    *refs,
):
    own, other = refs[:pieces], refs[pieces : 2 * pieces]
    keep_ref, send_ref, chosen_ref, table, grads, dq_ref, dk_ref, dv_ref = refs[2 * pieces :]
    core = core_ref[0]
    load_weights(core, own, other, table)
    tensor_size, types, per_shard, width, model = own[0].shape
    x = x_ref[...].astype(F32)
    chosen_grad = cg_ref[...].astype(F32)
    gate = gate_ref[...]
    attended = att_ref[...]
    middle = x + attended
    d_normed_two = dn_own[...] + dn_recv[...].astype(F32)
    scale_two = inv_rms(middle)
    grad_gain_two = jnp.sum(d_normed_two * middle * scale_two, 0, keepdims=True)
    weighted = d_normed_two * gain_two[...]
    d_middle = weighted * scale_two - middle * (
        scale_two * scale_two * scale_two * jnp.mean(weighted * middle, -1, keepdims=True)
    )
    d_attended = (d_middle + gate * chosen_grad).astype(BF16)
    grads[3] = tn(mixed_ref[...], d_attended).astype(BF16)
    d_mixed = nt(d_attended, table[3]).astype(BF16)
    allowed = allowed_mask(tag_col[...], tag_row[...])
    heads = q_ref.shape[1] // HD
    for h in range(heads):
        part = slice(h * HD, (h + 1) * HD)
        q, k, v = q_ref[:, part], k_ref[:, part], v_ref[:, part]
        dm = d_mixed[:, part]
        scores = jnp.where(allowed, nt(q, k) * HD**-0.5, NEG)
        probs = jnp.exp(scores - lse_ref[:, h : h + 1])
        d_probs = nt(dm, v)
        dv_ref[:, part] = tn(probs.astype(BF16), dm).astype(BF16)
        d_scores = probs * (d_probs - jnp.sum(d_probs * probs, -1, keepdims=True))
        d_scores = d_scores.astype(BF16)
        dq_ref[:, part] = (nn(d_scores, k) * HD**-0.5).astype(BF16)
        dk_ref[:, part] = (tn(d_scores, q) * HD**-0.5).astype(BF16)
    scale_one = inv_rms(x)
    normed = (x * scale_one * gain_one[...]).astype(BF16)
    grads[0] = tn(dq_ref[...], normed).astype(BF16)
    grads[1] = tn(dk_ref[...], normed).astype(BF16)
    grads[2] = tn(dv_ref[...], normed).astype(BF16)
    d_normed = nn(dq_ref[...], table[0]) + nn(dk_ref[...], table[1]) + nn(dv_ref[...], table[2])
    grad_gain_one = jnp.sum(d_normed * x * scale_one, 0, keepdims=True)
    weighted = d_normed * gain_one[...]
    d_first = weighted * scale_one - x * (
        scale_one * scale_one * scale_one * jnp.mean(weighted * x, -1, keepdims=True)
    )
    branch = br_own[...] + br_recv[...].astype(F32)
    d_gate = jnp.sum(chosen_grad * (attended + branch), -1, keepdims=True)
    chosen_ref[...] = (chosen_grad + d_middle + d_first + d_gate * router[...]).astype(BF16)
    grad_router = jnp.sum(d_gate * x, 0, keepdims=True)
    small = jnp.concatenate(
        [grad_router, grad_gain_one, grad_gain_two, jnp.zeros((EXTRA - 3, model), F32)], 0
    ).astype(BF16)
    body = tensor_size * types * per_shard * width
    for which, out in ((core, keep_ref), (1 - core, send_ref)):
        for c in range(pieces):
            for z in range(tensor_size):
                for t in range(types):
                    for h in range(per_shard):
                        source = (z * per_shard + h) * HD + c * width
                        start = ((z * types + t) * per_shard + h) * width
                        out[c, start : start + width, :] = grads[
                            2 * which + t, source : source + width, :
                        ]
            out[c, body : body + EXTRA, :] = small


def call(kernel, outs, args, scratch=(), flops=0, aliases=None):
    size = sum(a.size * a.dtype.itemsize for a in args) + sum(
        o.size * o.dtype.itemsize for o in outs
    )
    whole = pl.BlockSpec(memory_space=pltpu.VMEM)
    in_specs = [
        pl.BlockSpec(memory_space=pltpu.SMEM) if a.shape == (1,) else whole for a in args
    ]
    return pl.pallas_call(
        kernel,
        out_shape=outs,
        in_specs=in_specs,
        out_specs=[whole] * len(outs),
        scratch_shapes=scratch,
        input_output_aliases=aliases or {},
        compiler_params=pltpu.CompilerParams(vmem_limit_bytes=VMEM_LIMIT),
        cost_estimate=pl.CostEstimate(flops=flops, bytes_accessed=size, transcendentals=0),
    )(*args)


def local(
    dp_size,
    tensor_size,
    tokens,
    segment_ids,
    selected,
    w_router,
    gain_one,
    w_query,
    w_key,
    w_value,
    w_out,
    gain_two,
    w_up,
    w_down,
    grad_out,
):
    row_count, local_len, model = tokens.shape
    picks = selected.shape[1]
    full_len = segment_ids.shape[1]
    chips = dp_size // 2
    width = HD // chips
    per_shard = w_query.shape[1] // HD
    hidden_width = w_up.shape[1] // dp_size
    assert row_count == tensor_size and HD % chips == 0
    dp_index = lax.axis_index("dp")
    my_z = lax.axis_index("tensor")
    core, chip = dp_index % 2, dp_index // 2

    def to_core(values):
        return lax.ppermute(values, "dp", [(i, i ^ 1) for i in range(dp_size)])

    def to_chip(values, k):
        return lax.ppermute(values, "dp", [(i, i ^ (2 * k)) for i in range(dp_size)])

    def to_z(values, k):
        return lax.ppermute(values, "tensor", [(i, i ^ k) for i in range(tensor_size)])

    first = jnp.where(core == 0, w_query.T, w_value.T)
    second = jnp.where(core == 0, w_key.T, w_out)
    both = jnp.stack([first, second]).reshape(2, per_shard, chips, width, model)
    attn_mine = lax.dynamic_index_in_dim(both, chip, 2, keepdims=False)
    up_mine = lax.dynamic_slice_in_dim(w_up, dp_index * hidden_width, hidden_width, 1).T
    down_mine = lax.dynamic_slice_in_dim(w_down, dp_index * hidden_width, hidden_width, 0)
    ffn_mine = jnp.stack([up_mine, down_mine])

    attn_z = jnp.stack([attn_mine] + [to_z(attn_mine, k) for k in range(1, tensor_size)])
    ffn_z = jnp.stack([ffn_mine] + [to_z(ffn_mine, k) for k in range(1, tensor_size)])
    attn_own = [attn_z] + [to_chip(attn_z, k) for k in range(1, chips)]
    attn_oth = [to_core(piece) for piece in attn_own]
    ffn_own = [ffn_z] + [to_chip(ffn_z, k) for k in range(1, chips)]
    if width % 16:
        merge = lambda parts: jnp.stack(parts, 3).reshape(
            tensor_size, 2, per_shard, HD, model
        )
        attn_own, attn_oth = [merge(attn_own)], [merge(attn_oth)]
    step = 1
    while (hidden_width * step) % 16:
        step *= 2
    merged = [
        jnp.concatenate(ffn_own[i : i + step], 2) for i in range(0, chips, step)
    ]

    local_pos = my_z * local_len + jnp.arange(local_len, dtype=jnp.int32)
    hit = selected[:, :, None] == local_pos[None, None, :]
    hit_bf = hit.astype(BF16)

    def take(values):
        part = jnp.einsum("rkl,rld->rkd", hit_bf, values, preferred_element_type=F32)
        return lax.psum_scatter(part.astype(BF16), "tensor", scatter_dimension=0, tiled=True)[0]

    chosen = take(tokens)
    chosen_grad = take(grad_out)
    my_sel = lax.dynamic_index_in_dim(selected, my_z, 0, keepdims=False)
    my_seg = lax.dynamic_index_in_dim(segment_ids, my_z, 0, keepdims=False)
    full_pos = jnp.arange(full_len, dtype=jnp.int32)
    tags = jnp.sum(jnp.where(my_sel[:, None] == full_pos[None, :], my_seg[None, :], 0), 1)
    tag_col, tag_row = tags[:, None], tags[None, :]
    core_arr = core.reshape(1)
    g_one, g_two = gain_one[None, :], gain_two[None, :]
    router = w_router.astype(F32)[None, :]

    row_bf = jax.ShapeDtypeStruct((picks, model), BF16)
    row_f32 = jax.ShapeDtypeStruct((picks, model), F32)
    head_dims = per_shard * tensor_size * HD
    heads = per_shard * tensor_size
    table = pltpu.VMEM((4, head_dims, model), BF16)
    weights = attn_own + attn_oth
    q, k, v, mixed, lse, attended, normed_two, gate = call(
        functools.partial(attend_kernel, len(attn_own)),
        [row_bf] * 4
        + [jax.ShapeDtypeStruct((picks, heads), F32), row_f32, row_bf]
        + [jax.ShapeDtypeStruct((picks, 1), F32)],
        [core_arr, chosen, tag_col, tag_row, g_one, g_two, router] + weights,
        [table],
        flops=10 * picks * model * model,
    )

    d_branch = (gate * chosen_grad.astype(F32)).astype(BF16)
    n2_oth, db_oth = to_core(normed_two), to_core(d_branch)
    groups = 2 if len(merged) % 2 == 0 else 1
    per_call = len(merged) // groups
    acc, grad_pieces = [], []
    for g in range(groups):
        mine = merged[g * per_call : (g + 1) * per_call]
        last = g == groups - 1
        pair = jax.ShapeDtypeStruct((2 * picks, model), F32)
        outs = [jax.ShapeDtypeStruct(p.shape, BF16) for p in mine] + (
            [row_f32, row_bf] * 2 if last else [pair] * 2
        )
        results = call(
            functools.partial(hidden_kernel, per_call, g == 0, last),
            outs,
            [normed_two, n2_oth, d_branch, db_oth] + mine + acc,
            flops=12 * 2 * picks * model * mine[0].shape[2] * tensor_size * per_call,
        )
        grad_pieces += results[:per_call]
        acc = list(results[per_call:])
    dn_own, dn_send, br_own, br_send = acc
    if step > 1:
        grad_pieces = [
            p[:, :, i * hidden_width : (i + 1) * hidden_width]
            for p in grad_pieces
            for i in range(step)
        ]
    dn_recv, br_recv = to_core(dn_send), to_core(br_send)

    def total(parts):
        return sum(p.astype(F32) for p in parts).astype(BF16)

    ffn_sum = total([grad_pieces[0]] + [to_chip(grad_pieces[k], k) for k in range(1, chips)])
    ffn_sum = total([ffn_sum[0]] + [to_z(ffn_sum[k], k) for k in range(1, tensor_size)])
    ffn_all = lax.all_gather(ffn_sum, "dp", axis=0, tiled=False)
    grad_up = ffn_all[:, 0].reshape(w_up.shape[1], model).astype(F32).T
    grad_down = ffn_all[:, 1].reshape(w_up.shape[1], model).astype(F32)

    branch = br_own + br_recv.astype(F32)
    updated = (chosen.astype(F32) + gate * (attended + branch)).astype(BF16)
    updated_all = lax.all_gather(updated, "tensor", axis=0, tiled=False)

    covered = jnp.any(hit, axis=1)[:, :, None]

    def place(values, initial):
        placed = jnp.einsum("rkl,rkd->rld", hit_bf, values, preferred_element_type=F32)
        return jnp.where(covered, placed.astype(BF16), initial)

    layer_out = place(updated_all, tokens)

    piece_count = len(attn_own)
    body = tensor_size * 2 * per_shard * (HD // piece_count)
    packed = jax.ShapeDtypeStruct((piece_count, body + EXTRA, model), BF16)
    keep, send, d_chosen = call(
        functools.partial(back_kernel, piece_count),
        [packed, packed, row_bf],
        [core_arr, chosen, chosen_grad, gate, attended, br_own, br_recv, dn_own, dn_recv]
        + [q, k, v, mixed, lse, tag_col, tag_row, g_one, g_two, router]
        + weights,
        [table, table] + [pltpu.VMEM((picks, head_dims), BF16)] * 3,
        flops=20 * picks * model * model,
    )
    grad_all = lax.all_gather(d_chosen, "tensor", axis=0, tiled=False)
    grad_tokens = place(grad_all, grad_out)

    recv = to_core(send)
    if piece_count == chips:
        halves = [total([keep[k], recv[k]]) for k in range(chips)]
    else:
        both = total([keep[0], recv[0]])
        blocks = both[:body].reshape(-1, chips, width, model)
        halves = [
            jnp.concatenate([blocks[:, k].reshape(-1, model), both[body:]], 0)
            for k in range(chips)
        ]
    attn_sum = total([halves[0]] + [to_chip(halves[k], k) for k in range(1, chips)])
    part = 2 * per_shard * width
    shards = [
        jnp.concatenate(
            [attn_sum[k * part : (k + 1) * part], attn_sum[tensor_size * part :]], 0
        )
        for k in range(tensor_size)
    ]
    attn_sum = total([shards[0]] + [to_z(shards[k], k) for k in range(1, tensor_size)])
    small = attn_sum[part:].astype(F32)
    attn_all = lax.all_gather(attn_sum[:part], "dp", axis=0, tiled=False)
    attn_all = attn_all.reshape(chips, 2, 2, per_shard, width, model).transpose(1, 2, 3, 0, 4, 5)
    attn_all = attn_all.reshape(4, per_shard * HD, model).astype(F32)
    return (
        layer_out,
        grad_tokens,
        small[0],
        small[1],
        attn_all[0].T,
        attn_all[1].T,
        attn_all[2].T,
        attn_all[3],
        small[2],
        grad_up,
        grad_down,
    )


def solution(mesh):
    placed = (
        P("dp", "tensor", None),
        P("dp", None),
        P("dp", None),
        P(),
        P(),
        P(None, "tensor"),
        P(None, "tensor"),
        P(None, "tensor"),
        P("tensor", None),
        P(),
        P(None, "tensor"),
        P("tensor", None),
        P("dp", "tensor", None),
    )
    return jax.shard_map(
        functools.partial(local, mesh.shape["dp"], mesh.shape["tensor"]),
        mesh=mesh,
        in_specs=placed,
        out_specs=(
            P("dp", "tensor", None),
            P("dp", "tensor", None),
            P(),
            P(),
            P(None, "tensor"),
            P(None, "tensor"),
            P(None, "tensor"),
            P("tensor", None),
            P(),
            P(None, "tensor"),
            P("tensor", None),
        ),
        check_vma=False,
    )
```

```python
import functools

import jax
import jax.numpy as jnp
from jax import lax
from jax.experimental import pallas as pl
from jax.experimental.pallas import tpu as pltpu
from jax.sharding import PartitionSpec as P


HD = 64
EPS = 1e-06
NEG = -1e30
EXTRA = 16
CHIPS = 4
GROUP = 2 * CHIPS
DP = ("group", "chip", "core")
MIB = 1024 * 1024
F32 = jnp.float32
BF16 = jnp.bfloat16


def nn(left, right):
    return lax.dot_general(left, right, (((1,), (0,)), ((), ())), preferred_element_type=F32)


def nt(left, right):
    return lax.dot_general(left, right, (((1,), (1,)), ((), ())), preferred_element_type=F32)


def tn(left, right):
    return lax.dot_general(left, right, (((0,), (0,)), ((), ())), preferred_element_type=F32)


def inv_rms(values):
    return lax.rsqrt(jnp.mean(values * values, -1, keepdims=True) + EPS)


def load_weights(core, tensor_size, places, own, other, table):
    pieces = len(places)
    width = HD // pieces
    heads = table.shape[1] // (HD * tensor_size)
    for which, refs in ((core, own), (1 - core, other)):
        for c in range(pieces):
            for z in range(tensor_size):
                ref, base = places[c][z]
                for t in range(2):
                    for h in range(heads):
                        start = (z * heads + h) * HD + c * width
                        source = base + (t * heads + h) * width
                        table[2 * which + t, start : start + width, :] = refs[ref][
                            source : source + width, :
                        ]


def run_rows(start, count, room):
    row = lax.broadcasted_iota(jnp.int32, (count, room), 0)
    slot = lax.broadcasted_iota(jnp.int32, (count, room), 1)
    return (row == start + slot).astype(F32).astype(BF16)


def allowed_mask(tag_col, tag_row):
    count = tag_row.shape[1]
    query = lax.broadcasted_iota(jnp.int32, (count, count), 0)
    key = lax.broadcasted_iota(jnp.int32, (count, count), 1)
    return (tag_col == tag_row) & (query >= key)


def take_kernel(start_ref, picked_ref, tokens_ref, grads_ref, out_ref):
    length = tokens_ref.shape[1]
    room = picked_ref.shape[1]
    position = start_ref[0] + lax.broadcasted_iota(jnp.int32, (room, length), 1)
    hit = (picked_ref[0] == position).astype(F32).astype(BF16)
    out_ref[0, :room] = nn(hit, tokens_ref[0]).astype(BF16)
    out_ref[0, room:] = nn(hit, grads_ref[0]).astype(BF16)


def gate_of(chosen, router):
    return jnp.sum(chosen * router, -1, keepdims=True)


def gather_kernel(start_ref, router_ref, runs_ref, pair_ref, db_ref):
    count = db_ref.shape[0]
    room = runs_ref.shape[1] // 2
    chosen, grads = 0.0, 0.0
    for t in range(runs_ref.shape[0]):
        rows = run_rows(start_ref[t], count, room)
        chosen += nn(rows, runs_ref[t, :room])
        grads += nn(rows, runs_ref[t, room:])
    pair_ref[:count, :] = chosen.astype(BF16)
    pair_ref[count:, :] = grads.astype(BF16)
    db_ref[...] = (gate_of(chosen, router_ref[...]) * grads).astype(BF16)


def attend_kernel(
    tensor_size, places, arrays, core_ref, pair_ref, tag_col, tag_row, gain_one, gain_two, *refs
):
    own, other = refs[:arrays], refs[arrays : 2 * arrays]
    q_ref, k_ref, v_ref, mixed_ref, lse_ref, att_ref, normed_two_ref, table = refs[
        2 * arrays :
    ]
    count = pair_ref.shape[0] // 2
    load_weights(core_ref[0], tensor_size, places, own, other, table)
    x = pair_ref[:count, :].astype(F32)
    normed = (x * inv_rms(x) * gain_one[...]).astype(BF16)
    q_ref[...] = nt(normed, table[0]).astype(BF16)
    k_ref[...] = nt(normed, table[1]).astype(BF16)
    v_ref[...] = nt(normed, table[2]).astype(BF16)
    allowed = allowed_mask(tag_col[...], tag_row[...])
    heads = q_ref.shape[1] // HD
    for h in range(heads):
        part = slice(h * HD, (h + 1) * HD)
        scores = jnp.where(allowed, nt(q_ref[:, part], k_ref[:, part]) * HD**-0.5, NEG)
        top = jnp.max(scores, -1, keepdims=True)
        shifted = jnp.exp(scores - top)
        total = jnp.sum(shifted, -1, keepdims=True)
        probs = (shifted / total).astype(BF16)
        mixed_ref[:, part] = nn(probs, v_ref[:, part]).astype(BF16)
        lse_ref[:, h : h + 1] = top + jnp.log(total)
    attended = nn(mixed_ref[...], table[3])
    att_ref[...] = attended
    middle = x + attended
    normed_two_ref[...] = (middle * inv_rms(middle) * gain_two[...]).astype(BF16)


GELU_A = 0.7978845608028654
GELU_B = 0.044715


def gelu_parts(pre):
    inner = jnp.tanh(GELU_A * (pre + GELU_B * pre * pre * pre))
    return inner, (0.5 * pre * (1.0 + inner)).astype(BF16)


def side_weights(weights, side):
    width = weights.shape[1] // 2
    start = side * width
    return jnp.concatenate(
        [weights[z, start : start + width] for z in range(weights.shape[0])], 0
    )


def row_pair(refs, k):
    return jnp.concatenate([refs[k][...], refs[len(refs) // 2 + k][...]], 0)


def hidden_kernel(count, *refs):
    n2_refs, (weights, pre_ref, keep_ref, send_ref) = refs[:count], refs[count:]
    up, down = side_weights(weights, 0), side_weights(weights, 1)
    rows = n2_refs[0].shape[0]
    for k in range(count // 2):
        pre = nt(row_pair(n2_refs, k), up)
        pre_ref[k] = pre
        branch = nn(gelu_parts(pre)[1], down).astype(BF16)
        keep_ref[k], send_ref[k] = branch[:rows], branch[rows:]


def hidden_back_kernel(count, *refs):
    n2_refs, db_refs, refs = refs[:count], refs[count : 2 * count], refs[2 * count :]
    weights, pre_ref, refs = refs[0], refs[1], refs[2:]
    grads, keep_ref, sends = refs[: weights.shape[0]], refs[weights.shape[0]], refs[-CHIPS:]
    shards, width = weights.shape[0], weights.shape[1] // 2
    up, down = side_weights(weights, 0), side_weights(weights, 1)
    grad_up, grad_down = 0.0, 0.0
    rows = n2_refs[0].shape[0]
    for k in range(count // 2):
        n2, db = row_pair(n2_refs, k), row_pair(db_refs, k)
        pre = pre_ref[k]
        inner, hidden = gelu_parts(pre)
        slope = 0.5 * (1.0 + inner) + 0.5 * pre * (1.0 - inner * inner) * (
            GELU_A * (1.0 + 3.0 * GELU_B * pre * pre)
        )
        d_pre = (nt(db, down) * slope).astype(BF16)
        d_normed = nn(d_pre, up).astype(BF16)
        keep_ref[k], sends[k][...] = d_normed[:rows], d_normed[rows:]
        grad_up += tn(d_pre, n2)
        grad_down += tn(hidden, db)
    for z in range(shards):
        part = slice(z * width, (z + 1) * width)
        grads[z][:width, :] = grad_up[part].astype(BF16)
        grads[z][width:, :] = grad_down[part].astype(BF16)


def add_kernel(keep_ref, *refs):
    taken, outs = refs[:CHIPS], refs[CHIPS:]
    for k, out in enumerate(outs):
        out[...] = (keep_ref[k].astype(F32) + taken[k][...].astype(F32)).astype(out.dtype)


def add_stack_kernel(chip_ref, keep_ref, taken_ref, out_ref):
    for k in range(keep_ref.shape[0]):
        values = keep_ref[k].astype(F32) + taken_ref[k].astype(F32)
        out_ref[chip_ref[0] ^ k] = values.astype(BF16)


def total(refs):
    out = refs[0][...].astype(F32)
    for ref in refs[1:]:
        out = out + ref[...].astype(F32)
    return out


def sum_stack_kernel(parts_ref, out_ref):
    out_ref[...] = jnp.sum(parts_ref[...].astype(F32), 0).astype(BF16)


def sum_kernel(*refs):
    refs[-1][...] = total(refs[:-1]).astype(BF16)


def halves_kernel(keep_ref, taken_ref, small_own, small_oth, *outs):
    small = (small_own[...].astype(F32) + small_oth[...].astype(F32)).astype(BF16)
    body = keep_ref.shape[1]
    for k, out in enumerate(outs):
        out[:body, :] = (keep_ref[k].astype(F32) + taken_ref[k].astype(F32)).astype(BF16)
        out[body:, :] = small


def shards_kernel(count, *refs):
    values = total(refs[:count]).astype(BF16)
    outs = refs[count:]
    rows = outs[0].shape[0] - EXTRA
    for z, out in enumerate(outs):
        out[:rows, :] = values[z * rows : (z + 1) * rows]
        out[rows:, :] = values[len(outs) * rows :]


def back_kernel(
    tensor_size,
    places,
    arrays,
    core_ref,
    start_ref,
    pair_ref,
    att_ref,
    q_ref,
    k_ref,
    v_ref,
    mixed_ref,
    lse_ref,
    tag_col,
    tag_row,
    gain_one,
    gain_two,
    router,
    *refs,
):
    own, other = refs[:arrays], refs[arrays : 2 * arrays]
    refs = refs[2 * arrays :]
    d_norms, branch_ref, refs = refs[:CHIPS], refs[CHIPS], refs[CHIPS + 1 :]
    keep_ref, send_ref, small_ref, out_ref, updated_ref, chosen_ref = refs[:6]
    table, grads, dq_ref, dk_ref, dv_ref = refs[6:]
    core = core_ref[0]
    load_weights(core, tensor_size, places, own, other, table)
    pieces = len(places)
    types, width = 2, HD // pieces
    count, model = pair_ref.shape[0] // 2, pair_ref.shape[1]
    per_shard = table.shape[1] // (HD * tensor_size)
    x = pair_ref[:count, :].astype(F32)
    chosen_grad = pair_ref[count:, :].astype(F32)
    gate = gate_of(x, router[...])
    attended = att_ref[...]
    middle = x + attended
    d_normed_two = total(d_norms)
    scale_two = inv_rms(middle)
    grad_gain_two = jnp.sum(d_normed_two * middle * scale_two, 0, keepdims=True)
    weighted = d_normed_two * gain_two[...]
    d_middle = weighted * scale_two - middle * (
        scale_two * scale_two * scale_two * jnp.mean(weighted * middle, -1, keepdims=True)
    )
    d_attended = (d_middle + gate * chosen_grad).astype(BF16)
    grads[3] = tn(mixed_ref[...], d_attended).astype(BF16)
    d_mixed = nt(d_attended, table[3]).astype(BF16)
    allowed = allowed_mask(tag_col[...], tag_row[...])
    heads = q_ref.shape[1] // HD
    for h in range(heads):
        part = slice(h * HD, (h + 1) * HD)
        q, k, v = q_ref[:, part], k_ref[:, part], v_ref[:, part]
        dm = d_mixed[:, part]
        scores = jnp.where(allowed, nt(q, k) * HD**-0.5, NEG)
        probs = jnp.exp(scores - lse_ref[:, h : h + 1])
        d_probs = nt(dm, v)
        dv_ref[:, part] = tn(probs.astype(BF16), dm).astype(BF16)
        d_scores = probs * (d_probs - jnp.sum(d_probs * probs, -1, keepdims=True))
        d_scores = d_scores.astype(BF16)
        dq_ref[:, part] = (nn(d_scores, k) * HD**-0.5).astype(BF16)
        dk_ref[:, part] = (tn(d_scores, q) * HD**-0.5).astype(BF16)
    scale_one = inv_rms(x)
    normed = (x * scale_one * gain_one[...]).astype(BF16)
    grads[0] = tn(dq_ref[...], normed).astype(BF16)
    grads[1] = tn(dk_ref[...], normed).astype(BF16)
    grads[2] = tn(dv_ref[...], normed).astype(BF16)
    d_normed = nn(dq_ref[...], table[0]) + nn(dk_ref[...], table[1]) + nn(dv_ref[...], table[2])
    grad_gain_one = jnp.sum(d_normed * x * scale_one, 0, keepdims=True)
    weighted = d_normed * gain_one[...]
    d_first = weighted * scale_one - x * (
        scale_one * scale_one * scale_one * jnp.mean(weighted * x, -1, keepdims=True)
    )
    delta = attended + jnp.sum(branch_ref[...].astype(F32), 0)
    updated_ref[...] = (x + gate * delta).astype(BF16)
    d_gate = jnp.sum(chosen_grad * delta, -1, keepdims=True)
    chosen_ref[...] = (chosen_grad + d_middle + d_first + d_gate * router[...]).astype(BF16)
    room = out_ref.shape[1] // 2
    for t in range(tensor_size):
        rows = run_rows(start_ref[t], count, room)
        out_ref[t, :room] = tn(rows, updated_ref[...]).astype(BF16)
        out_ref[t, room:] = tn(rows, chosen_ref[...]).astype(BF16)
    grad_router = jnp.sum(d_gate * x, 0, keepdims=True)
    small_ref[...] = jnp.concatenate(
        [grad_router, grad_gain_one, grad_gain_two, jnp.zeros((EXTRA - 3, model), F32)], 0
    ).astype(BF16)
    for which, out in ((core, keep_ref), (1 - core, send_ref)):
        for c in range(pieces):
            for z in range(tensor_size):
                for t in range(types):
                    for h in range(per_shard):
                        source = (z * per_shard + h) * HD + c * width
                        start = ((z * types + t) * per_shard + h) * width
                        out[c, start : start + width, :] = grads[
                            2 * which + t, source : source + width, :
                        ]


def hidden_finish_kernel(pieces, place_ref, *refs):
    up_ref, down_ref, up_rows = refs[2 * pieces :]
    chip, core = place_ref[0], place_ref[1]
    width = refs[0].shape[0] // 2
    for side in range(2):
        for k in range(pieces):
            piece = refs[side * pieces + k]
            source = 2 * (chip ^ k) + (core ^ side)
            rows = pl.ds(pl.multiple_of(source * width, width), width)
            up_rows[rows, :] = piece[:width, :].astype(F32)
            down_ref[rows, :] = piece[width:, :].astype(F32)
    up_ref[...] = up_rows[...].T


def attn_finish_kernel(pieces, place_ref, *refs):
    query_ref, key_ref, value_ref, out_ref, table = refs[2 * pieces :]
    chip, core = place_ref[0], place_ref[1]
    heads = query_ref.shape[0] // HD
    width = HD // pieces
    for side in range(2):
        for k in range(pieces):
            piece = refs[side * pieces + k]
            for t in range(2):
                for h in range(heads):
                    start = (t * heads + h) * width
                    rows = pl.ds(pl.multiple_of(h * HD + (chip ^ k) * width, width), width)
                    table[2 * (core ^ side) + t, rows, :] = piece[
                        start : start + width, :
                    ].astype(F32)
    for t, ref in enumerate((query_ref, key_ref, value_ref, out_ref)):
        ref[...] = table[t]


def join_kernel(*refs):
    start = 0
    for ref in refs[:-1]:
        rows = ref.shape[0]
        refs[-1][start : start + rows, :] = ref[...]
        start += rows


def flag_kernel(*refs):
    top = refs[0][...].astype(F32)
    for ref in refs[1:-1]:
        top = jnp.maximum(top, ref[...].astype(F32))
    refs[-1][0] = jnp.max(top)


FREE = pl.CostEstimate(flops=1, bytes_accessed=1, transcendentals=0)


def call(kernel, outs, args, scratch=(), limit=16 * MIB):
    whole = pl.BlockSpec(memory_space=pltpu.VMEM)
    in_specs = [
        pl.BlockSpec(memory_space=pltpu.SMEM) if a.ndim == 1 else whole for a in args
    ]
    return pl.pallas_call(
        kernel,
        out_shape=outs,
        in_specs=in_specs,
        out_specs=[whole] * len(outs),
        scratch_shapes=scratch,
        compiler_params=pltpu.CompilerParams(vmem_limit_bytes=limit),
        cost_estimate=FREE,
    )(*args)


def join(*parts):
    rows = sum(p.shape[0] for p in parts)
    shape = jax.ShapeDtypeStruct((rows, parts[0].shape[1]), parts[0].dtype)
    return call(join_kernel, [shape], list(parts))[0]


def local(
    dp_size,
    tensor_size,
    tokens,
    segment_ids,
    selected,
    w_router,
    gain_one,
    w_query,
    w_key,
    w_value,
    w_out,
    gain_two,
    w_up,
    w_down,
    grad_out,
):
    row_count, local_len, model = tokens.shape
    picks = selected.shape[1]
    full_len = segment_ids.shape[1]
    width = HD // CHIPS
    per_shard = w_query.shape[1] // HD
    hidden_count = w_up.shape[1]
    hidden_width = hidden_count // GROUP
    assert row_count == tensor_size and dp_size % GROUP == 0
    dp_index = lax.axis_index(DP)
    my_z = lax.axis_index("tensor")
    member = dp_index % GROUP
    core, chip = member % 2, member // 2
    tie = lax.optimization_barrier

    def to_peer(values, step):
        return lax.ppermute(values, DP, [(i, i ^ step) for i in range(dp_size)])

    def to_core(values):
        return to_peer(values, 1)

    def to_chip(values, k):
        return to_peer(values, 2 * k)

    def to_z(values, k):
        return lax.ppermute(values, "tensor", [(i, i ^ k) for i in range(tensor_size)])

    def over_z(values):
        return [values] + [to_z(values, k) for k in range(1, tensor_size)]

    def over_chips(values):
        return [values] + [to_chip(values, k) for k in range(1, CHIPS)]

    def over_group(values):
        own = over_chips(values)
        return own + [to_core(v) for v in own]

    def row_of(values, k):
        return lax.dynamic_index_in_dim(values, my_z ^ k, 0, keepdims=False)

    def trade_z(parts):
        return [parts[0]] + [to_z(parts[k], k) for k in range(1, tensor_size)]

    def trade_shards(parts):
        stack = jnp.stack(parts)
        return trade_z([row_of(stack, k) for k in range(tensor_size)])

    def trade_chips(parts):
        return [parts[0]] + [to_chip(parts[k], k) for k in range(1, CHIPS)]

    def all_z(values):
        return lax.all_to_all(values, "tensor", 0, 0, tiled=True)

    def shape(*dims, dtype=BF16):
        return jax.ShapeDtypeStruct(dims, dtype)

    def summed(parts):
        return call(sum_kernel, [shape(*parts[0].shape)], parts)[0]

    def over_groups(values):
        step = GROUP
        while step < dp_size:
            values = summed([values, to_peer(values, step)])
            step *= 2
        return values

    row_bf, row_f32 = shape(picks, model), shape(picks, model, dtype=F32)

    def chip_rows(values):
        values = values.reshape(per_shard, CHIPS, width, model)
        return lax.dynamic_index_in_dim(values, chip, 1, keepdims=False)

    first = jnp.where(core == 0, chip_rows(w_query.T), chip_rows(w_value.T))
    second = jnp.where(core == 0, chip_rows(w_key.T), chip_rows(w_out))
    attn_mine = jnp.stack([first, second]).reshape(2 * per_shard * width, model)
    attn_parts = over_z(attn_mine)
    up_mine = lax.dynamic_slice_in_dim(w_up, member * hidden_width, hidden_width, 1)
    down_mine = lax.dynamic_slice_in_dim(w_down, member * hidden_width, hidden_width, 0)
    up_mine, down_mine = tie((up_mine, down_mine))
    ffn_mine = jnp.concatenate([up_mine.T, down_mine], 0)

    room = 3 * picks // (2 * tensor_size)
    local_start = my_z * local_len
    order = jnp.arange(picks, dtype=jnp.int32)
    slot = jnp.arange(room, dtype=jnp.int32)
    edges = jnp.arange(tensor_size + 1, dtype=jnp.int32) * local_len
    counts = jnp.sum((selected[:, None, :] < edges[None, :, None]).astype(jnp.int32), -1)
    most = jnp.max(counts[:, 1:] - counts[:, :-1]).astype(BF16)
    run_start = jnp.sum((selected < local_start).astype(jnp.int32), 1)
    window = order[None, None, :] == run_start[:, None, None] + slot[None, :, None]
    picked = jnp.sum(jnp.where(window, selected[:, None, :] + 1, 0), -1) - 1
    my_sel = lax.dynamic_index_in_dim(selected, my_z, 0, keepdims=False)
    my_seg = lax.dynamic_index_in_dim(segment_ids, my_z, 0, keepdims=False)
    start_all = jnp.sum((my_sel[None, :] < edges[:-1, None]).astype(jnp.int32), -1)
    full_pos = jnp.arange(full_len, dtype=jnp.int32)
    tags = jnp.sum(jnp.where(my_sel[:, None] == full_pos[None, :], my_seg[None, :], 0), 1)
    tag_col, tag_row = tags[:, None], tags[None, :]
    core_arr = core.reshape(1)
    g_one, g_two = gain_one[None, :], gain_two[None, :]
    router = w_router.astype(F32)[None, :]

    runs = pl.pallas_call(
        take_kernel,
        out_shape=shape(row_count, 2 * room, model),
        grid=(row_count,),
        in_specs=[
            pl.BlockSpec(memory_space=pltpu.SMEM),
            pl.BlockSpec((1, room, 1), lambda r: (r, 0, 0)),
            pl.BlockSpec((1, local_len, model), lambda r: (r, 0, 0)),
            pl.BlockSpec((1, local_len, model), lambda r: (r, 0, 0)),
        ],
        out_specs=pl.BlockSpec((1, 2 * room, model), lambda r: (r, 0, 0)),
        compiler_params=pltpu.CompilerParams(vmem_limit_bytes=16 * MIB),
        cost_estimate=FREE,
    )(local_start.reshape(1), picked[:, :, None], tokens, grad_out)
    ffn_all = jnp.broadcast_to(ffn_mine[None], (tensor_size, *ffn_mine.shape))
    small_inputs = (tag_col, tag_row, g_one, g_two, router, start_all, ffn_all)
    runs, attn_parts, small_inputs = tie((runs, attn_parts, small_inputs))
    tag_col, tag_row, g_one, g_two, router, start_all, ffn_all = small_inputs
    runs = all_z(runs)

    flag = jnp.full((EXTRA, model), most, BF16)
    half, part = tensor_size // 2, attn_mine.shape[0]
    first, second = join(*attn_parts[:half], flag), join(*attn_parts[half:])
    first = join(first, to_chip(first, 1))
    second = join(second, to_chip(second, 2))
    attn_own = [first, second, to_chip(first, 2), to_chip(second, 1)]
    places = [[None] * tensor_size for _ in range(CHIPS)]
    for c in range(CHIPS):
        for z in range(half):
            places[c][z] = (2 * (c // 2), (c % 2) * (half * part + EXTRA) + z * part)
            places[c][half + z] = (1 + 2 * (c % 2), (c // 2) * half * part + z * part)
    attn_oth = [to_core(piece) for piece in attn_own]
    attn_own, attn_oth = tie((attn_own, attn_oth))
    flags = [(i, row) for i in (0, 2) for row in (half * part, 2 * half * part + EXTRA)]
    most = pl.pallas_call(
        flag_kernel,
        out_shape=jax.ShapeDtypeStruct((1,), F32),
        grid=(1,),
        in_specs=[
            pl.BlockSpec((EXTRA, 128), lambda i, at=row // EXTRA: (at, 0)) for _, row in flags
        ]
        * 2,
        out_specs=pl.BlockSpec(memory_space=pltpu.SMEM),
        cost_estimate=FREE,
    )(*[side[i] for side in (attn_own, attn_oth) for i, _ in flags])
    step = GROUP
    while step < dp_size:
        most = jnp.maximum(most, to_peer(most, step))
        step *= 2
    crowded = most[0] > room


    local_pos = local_start + jnp.arange(local_len, dtype=jnp.int32)

    def dense_hit():
        return (selected[:, :, None] == local_pos[None, None, :]).astype(BF16)

    def take_dense(values):
        whole = jnp.einsum("rkl,rld->rkd", dense_hit(), values, preferred_element_type=F32)
        whole = whole.astype(BF16)
        return sum(trade_z([row_of(whole, k) for k in range(tensor_size)]))

    def gather_dense():
        chosen, grads = take_dense(tokens), take_dense(grad_out)
        scaled = gate_of(chosen.astype(F32), router) * grads.astype(F32)
        return [jnp.concatenate([chosen, grads], 0), scaled.astype(BF16)]

    pair, d_branch = lax.cond(
        crowded,
        gather_dense,
        lambda: list(
            call(gather_kernel, [shape(2 * picks, model), row_bf], [start_all, router, runs])
        ),
    )
    ffn_all, pair, d_branch = tie((ffn_all, pair, d_branch))
    d_branch_all = over_chips(d_branch)
    ffn_z = all_z(ffn_all)

    heads = per_shard * tensor_size
    head_dims = heads * HD
    table = pltpu.VMEM((4, head_dims, model), BF16)
    weights = attn_own + attn_oth
    q, k, v, mixed, lse, attended, normed_two = call(
        functools.partial(attend_kernel, tensor_size, places, len(attn_own)),
        [row_bf] * 4 + [shape(picks, heads, dtype=F32), row_f32, row_bf],
        [core_arr, pair, tag_col, tag_row, g_one, g_two] + weights,
        [table],
        limit=56 * MIB,
    )
    normed_two, d_branch_all = tie((normed_two, d_branch_all))
    d_branch_all = d_branch_all + [to_core(v) for v in d_branch_all]
    normed_two_all = over_group(normed_two)

    block = shape(CHIPS, picks, model)
    pre, br_keep, br_send = call(
        functools.partial(hidden_kernel, GROUP),
        [shape(CHIPS, 2 * picks, tensor_size * hidden_width, dtype=F32), block, block],
        normed_two_all + [ffn_z],
        limit=56 * MIB,
    )
    chip_arr = chip.reshape(1)
    branches = call(add_stack_kernel, [block], [chip_arr, br_keep, to_core(br_send)])[0]
    branches = lax.all_to_all(branches, "chip", 0, 0, tiled=True)
    results = call(
        functools.partial(hidden_back_kernel, GROUP),
        [shape(*ffn_mine.shape)] * tensor_size + [block] + [row_bf] * CHIPS,
        normed_two_all + d_branch_all + [ffn_z, pre],
        limit=56 * MIB,
    )
    ffn_grads, dn_keep, dn_send = results[:tensor_size], results[tensor_size], results[-CHIPS:]
    outs = [row_f32] + [row_bf] * (CHIPS - 1)
    d_norms = call(add_kernel, outs, [dn_keep] + [to_core(v) for v in dn_send])
    d_norms = trade_chips(list(d_norms))
    ffn_grads = trade_shards(ffn_grads)
    d_norms, ffn_grads[1], ffn_grads[2] = tie((d_norms, ffn_grads[1], ffn_grads[2]))

    body = tensor_size * 2 * per_shard * width
    packed = shape(CHIPS, body, model)
    keep, give, small, out_runs, updated, d_chosen = call(
        functools.partial(back_kernel, tensor_size, places, len(attn_own)),
        [packed, packed, shape(EXTRA, model), shape(tensor_size, 2 * room, model)]
        + [row_bf, row_bf],
        [core_arr, start_all, pair, attended, q, k, v, mixed, lse]
        + [tag_col, tag_row, g_one, g_two, router]
        + weights
        + d_norms
        + [branches],
        [table, table] + [pltpu.VMEM((picks, head_dims), BF16)] * 3,
        limit=56 * MIB,
    )
    halves = call(
        halves_kernel,
        [shape(body + EXTRA, model)] * CHIPS,
        [keep, to_core(give), small, to_core(small)],
    )
    attn_recv = trade_chips(list(halves))
    attn_recv, ffn_grads[3] = tie((attn_recv, ffn_grads[3]))
    out_runs = all_z(out_runs)

    ffn_sum = over_groups(summed(ffn_grads))
    place_arr = jnp.stack([chip, core])
    shards = call(
        functools.partial(shards_kernel, CHIPS),
        [shape(part + EXTRA, model)] * tensor_size,
        attn_recv,
    )
    shards, ffn_sum, out_runs = tie((shards, ffn_sum, out_runs))
    ffn_last = [ffn_sum, to_chip(ffn_sum, 1), to_chip(ffn_sum, 2)]
    z_recv = trade_z(shards)

    def place(hits, values, initial):
        covered = jnp.any(hits > 0, axis=1)[:, :, None]
        placed = jnp.einsum("rkl,rkd->rld", hits, values, preferred_element_type=F32)
        return jnp.where(covered, placed.astype(BF16), initial)

    def place_dense(values, initial):
        parts = [lax.all_gather(v, "tensor", axis=0) for v in jnp.split(values, 2, 0)]
        return place(dense_hit(), jnp.concatenate(parts, 1), initial)

    def place_runs():
        run_hit = (picked[:, :, None] == local_pos[None, None, :]).astype(BF16)
        return (
            place(run_hit, out_runs[:, :room], tokens),
            place(run_hit, out_runs[:, room:], grad_out),
        )

    layer_out, grad_tokens = lax.cond(
        crowded,
        lambda: (place_dense(updated, tokens), place_dense(d_chosen, grad_out)),
        place_runs,
    )

    z_recv, layer_out, grad_tokens = tie((z_recv, layer_out, grad_tokens))
    attn_sum = over_groups(summed(z_recv))
    ffn_sum, attn_sum = tie((ffn_sum, attn_sum))
    ffn_last.append(to_chip(ffn_sum, 3))
    ffn_last = ffn_last + [to_core(v) for v in ffn_last]
    square = shape(hidden_count, model, dtype=F32)
    grad_up, grad_down = call(
        functools.partial(hidden_finish_kernel, CHIPS),
        [shape(model, hidden_count, dtype=F32), square],
        [place_arr] + ffn_last,
        [pltpu.VMEM(square.shape, F32)],
    )

    small = attn_sum[part:].astype(F32)
    table_shape = (4, per_shard * HD, model)
    attn_all = call(
        functools.partial(attn_finish_kernel, CHIPS),
        [shape(*table_shape[1:], dtype=F32)] * 4,
        [place_arr] + over_group(attn_sum[:part]),
        [pltpu.VMEM(table_shape, F32)],
    )
    return (
        layer_out,
        grad_tokens,
        small[0],
        small[1],
        attn_all[0].T,
        attn_all[1].T,
        attn_all[2].T,
        attn_all[3],
        small[2],
        grad_up,
        grad_down,
    )


def solution(mesh):
    groups, tensor_size = mesh.shape["dp"] // GROUP, mesh.shape["tensor"]
    split = jax.sharding.Mesh(
        mesh.devices.reshape(groups, CHIPS, 2, tensor_size), (*DP, "tensor")
    )
    tokens, picks = P(DP, "tensor", None), P(DP, None)
    columns, rows = P(None, "tensor"), P("tensor", None)
    weights = (columns, columns, columns, rows, P(), columns, rows)
    return jax.shard_map(
        functools.partial(local, mesh.shape["dp"], tensor_size),
        mesh=split,
        in_specs=(tokens, picks, picks, P(), P(), *weights, tokens),
        out_specs=(tokens, tokens, P(), P(), *weights),
        check_vma=False,
    )
```

```python
import functools

import jax
import jax.numpy as jnp
from jax import lax
from jax.experimental import pallas as pl
from jax.experimental.pallas import tpu as pltpu
from jax.sharding import PartitionSpec as P


HD = 64
EPS = 1e-06
NEG = -1e30
EXTRA = 16
CHIPS = 4
GROUP = 2 * CHIPS
DP = ("group", "chip", "core")
MIB = 1024 * 1024
F32 = jnp.float32
BF16 = jnp.bfloat16


def nn(left, right):
    return lax.dot_general(left, right, (((1,), (0,)), ((), ())), preferred_element_type=F32)


def nt(left, right):
    return lax.dot_general(left, right, (((1,), (1,)), ((), ())), preferred_element_type=F32)


def tn(left, right):
    return lax.dot_general(left, right, (((0,), (0,)), ((), ())), preferred_element_type=F32)


def inv_rms(values):
    return lax.rsqrt(jnp.mean(values * values, -1, keepdims=True) + EPS)


def load_weights(core, tensor_size, places, own, other, table):
    pieces = len(places)
    width = HD // pieces
    heads = table.shape[1] // (HD * tensor_size)
    for which, refs in ((core, own), (1 - core, other)):
        for c in range(pieces):
            for z in range(tensor_size):
                ref, base = places[c][z]
                for t in range(2):
                    for h in range(heads):
                        start = (z * heads + h) * HD + c * width
                        source = base + (t * heads + h) * width
                        table[2 * which + t, start : start + width, :] = refs[ref][
                            source : source + width, :
                        ]


def run_rows(start, count, room):
    row = lax.broadcasted_iota(jnp.int32, (count, room), 0)
    slot = lax.broadcasted_iota(jnp.int32, (count, room), 1)
    return (row == start + slot).astype(F32).astype(BF16)


def allowed_mask(tag_col, tag_row):
    count = tag_row.shape[1]
    query = lax.broadcasted_iota(jnp.int32, (count, count), 0)
    key = lax.broadcasted_iota(jnp.int32, (count, count), 1)
    return (tag_col == tag_row) & (query >= key)


def take_kernel(start_ref, picked_ref, tokens_ref, grads_ref, out_ref):
    length = tokens_ref.shape[1]
    room = picked_ref.shape[1]
    position = start_ref[0] + lax.broadcasted_iota(jnp.int32, (room, length), 1)
    hit = (picked_ref[0] == position).astype(F32).astype(BF16)
    out_ref[0, :room] = nn(hit, tokens_ref[0]).astype(BF16)
    out_ref[0, room:] = nn(hit, grads_ref[0]).astype(BF16)


def gate_of(chosen, router):
    return jnp.sum(chosen * router, -1, keepdims=True)


def gather_kernel(start_ref, router_ref, runs_ref, pair_ref, db_ref):
    count = db_ref.shape[0]
    room = runs_ref.shape[1] // 2
    chosen, grads = 0.0, 0.0
    for t in range(runs_ref.shape[0]):
        rows = run_rows(start_ref[t], count, room)
        chosen += nn(rows, runs_ref[t, :room])
        grads += nn(rows, runs_ref[t, room:])
    pair_ref[:count, :] = chosen.astype(BF16)
    pair_ref[count:, :] = grads.astype(BF16)
    db_ref[...] = (gate_of(chosen, router_ref[...]) * grads).astype(BF16)


def attend_kernel(
    tensor_size, places, arrays, core_ref, pair_ref, tag_col, tag_row, gain_one, gain_two, *refs
):
    own, other = refs[:arrays], refs[arrays : 2 * arrays]
    q_ref, k_ref, v_ref, mixed_ref, lse_ref, att_ref, normed_two_ref, table = refs[
        2 * arrays :
    ]
    count = pair_ref.shape[0] // 2
    load_weights(core_ref[0], tensor_size, places, own, other, table)
    x = pair_ref[:count, :].astype(F32)
    normed = (x * inv_rms(x) * gain_one[...]).astype(BF16)
    q_ref[...] = nt(normed, table[0]).astype(BF16)
    k_ref[...] = nt(normed, table[1]).astype(BF16)
    v_ref[...] = nt(normed, table[2]).astype(BF16)
    allowed = allowed_mask(tag_col[...], tag_row[...])
    heads = q_ref.shape[1] // HD
    for h in range(heads):
        part = slice(h * HD, (h + 1) * HD)
        scores = jnp.where(allowed, nt(q_ref[:, part], k_ref[:, part]) * HD**-0.5, NEG)
        top = jnp.max(scores, -1, keepdims=True)
        shifted = jnp.exp(scores - top)
        total = jnp.sum(shifted, -1, keepdims=True)
        probs = (shifted / total).astype(BF16)
        mixed_ref[:, part] = nn(probs, v_ref[:, part]).astype(BF16)
        lse_ref[:, h : h + 1] = top + jnp.log(total)
    attended = nn(mixed_ref[...], table[3])
    att_ref[...] = attended
    middle = x + attended
    normed_two_ref[...] = (middle * inv_rms(middle) * gain_two[...]).astype(BF16)


GELU_A = 0.7978845608028654
GELU_B = 0.044715


def gelu_parts(pre):
    inner = jnp.tanh(GELU_A * (pre + GELU_B * pre * pre * pre))
    return inner, (0.5 * pre * (1.0 + inner)).astype(BF16)


def side_weights(weights, side):
    width = weights.shape[1] // 2
    start = side * width
    return jnp.concatenate(
        [weights[z, start : start + width] for z in range(weights.shape[0])], 0
    )


def row_pair(refs, k):
    return jnp.concatenate([refs[k][...], refs[len(refs) // 2 + k][...]], 0)


def hidden_kernel(count, *refs):
    n2_refs, (weights, pre_ref, keep_ref, send_ref) = refs[:count], refs[count:]
    up, down = side_weights(weights, 0), side_weights(weights, 1)
    rows = n2_refs[0].shape[0]
    for k in range(count // 2):
        pre = nt(row_pair(n2_refs, k), up)
        pre_ref[k] = pre
        branch = nn(gelu_parts(pre)[1], down).astype(BF16)
        keep_ref[k], send_ref[k] = branch[:rows], branch[rows:]


def hidden_back_kernel(count, *refs):
    n2_refs, db_refs, refs = refs[:count], refs[count : 2 * count], refs[2 * count :]
    weights, pre_ref, refs = refs[0], refs[1], refs[2:]
    grads, keep_ref, sends = refs[: weights.shape[0]], refs[weights.shape[0]], refs[-CHIPS:]
    shards, width = weights.shape[0], weights.shape[1] // 2
    up, down = side_weights(weights, 0), side_weights(weights, 1)
    grad_up, grad_down = 0.0, 0.0
    rows = n2_refs[0].shape[0]
    for k in range(count // 2):
        n2, db = row_pair(n2_refs, k), row_pair(db_refs, k)
        pre = pre_ref[k]
        inner, hidden = gelu_parts(pre)
        slope = 0.5 * (1.0 + inner) + 0.5 * pre * (1.0 - inner * inner) * (
            GELU_A * (1.0 + 3.0 * GELU_B * pre * pre)
        )
        d_pre = (nt(db, down) * slope).astype(BF16)
        d_normed = nn(d_pre, up).astype(BF16)
        keep_ref[k], sends[k][...] = d_normed[:rows], d_normed[rows:]
        grad_up += tn(d_pre, n2)
        grad_down += tn(hidden, db)
    for z in range(shards):
        part = slice(z * width, (z + 1) * width)
        grads[z][:width, :] = grad_up[part].astype(BF16)
        grads[z][width:, :] = grad_down[part].astype(BF16)


def add_kernel(keep_ref, *refs):
    taken, outs = refs[:CHIPS], refs[CHIPS:]
    for k, out in enumerate(outs):
        out[...] = (keep_ref[k].astype(F32) + taken[k][...].astype(F32)).astype(out.dtype)


def add_stack_kernel(chip_ref, keep_ref, taken_ref, out_ref):
    for k in range(keep_ref.shape[0]):
        values = keep_ref[k].astype(F32) + taken_ref[k].astype(F32)
        out_ref[chip_ref[0] ^ k] = values.astype(BF16)


def total(refs):
    out = refs[0][...].astype(F32)
    for ref in refs[1:]:
        out = out + ref[...].astype(F32)
    return out


def sum_stack_kernel(parts_ref, out_ref):
    out_ref[...] = jnp.sum(parts_ref[...].astype(F32), 0).astype(BF16)


def sum_kernel(*refs):
    refs[-1][...] = total(refs[:-1]).astype(BF16)


def halves_kernel(keep_ref, taken_ref, small_own, small_oth, *outs):
    small = (small_own[...].astype(F32) + small_oth[...].astype(F32)).astype(BF16)
    body = keep_ref.shape[1]
    for k, out in enumerate(outs):
        out[:body, :] = (keep_ref[k].astype(F32) + taken_ref[k].astype(F32)).astype(BF16)
        out[body:, :] = small


def shards_kernel(count, *refs):
    values = total(refs[:count]).astype(BF16)
    outs = refs[count:]
    rows = outs[0].shape[0] - EXTRA
    for z, out in enumerate(outs):
        out[:rows, :] = values[z * rows : (z + 1) * rows]
        out[rows:, :] = values[len(outs) * rows :]


def back_kernel(
    tensor_size,
    places,
    arrays,
    core_ref,
    start_ref,
    pair_ref,
    att_ref,
    q_ref,
    k_ref,
    v_ref,
    mixed_ref,
    lse_ref,
    tag_col,
    tag_row,
    gain_one,
    gain_two,
    router,
    *refs,
):
    own, other = refs[:arrays], refs[arrays : 2 * arrays]
    refs = refs[2 * arrays :]
    d_norms, branch_ref, refs = refs[:CHIPS], refs[CHIPS], refs[CHIPS + 1 :]
    keep_ref, send_ref, small_ref, out_ref, updated_ref, chosen_ref = refs[:6]
    table, grads, dq_ref, dk_ref, dv_ref = refs[6:]
    core = core_ref[0]
    load_weights(core, tensor_size, places, own, other, table)
    pieces = len(places)
    types, width = 2, HD // pieces
    count, model = pair_ref.shape[0] // 2, pair_ref.shape[1]
    per_shard = table.shape[1] // (HD * tensor_size)
    x = pair_ref[:count, :].astype(F32)
    chosen_grad = pair_ref[count:, :].astype(F32)
    gate = gate_of(x, router[...])
    attended = att_ref[...]
    middle = x + attended
    d_normed_two = total(d_norms)
    scale_two = inv_rms(middle)
    grad_gain_two = jnp.sum(d_normed_two * middle * scale_two, 0, keepdims=True)
    weighted = d_normed_two * gain_two[...]
    d_middle = weighted * scale_two - middle * (
        scale_two * scale_two * scale_two * jnp.mean(weighted * middle, -1, keepdims=True)
    )
    d_attended = (d_middle + gate * chosen_grad).astype(BF16)
    grads[3] = tn(mixed_ref[...], d_attended).astype(BF16)
    d_mixed = nt(d_attended, table[3]).astype(BF16)
    allowed = allowed_mask(tag_col[...], tag_row[...])
    heads = q_ref.shape[1] // HD
    for h in range(heads):
        part = slice(h * HD, (h + 1) * HD)
        q, k, v = q_ref[:, part], k_ref[:, part], v_ref[:, part]
        dm = d_mixed[:, part]
        scores = jnp.where(allowed, nt(q, k) * HD**-0.5, NEG)
        probs = jnp.exp(scores - lse_ref[:, h : h + 1])
        d_probs = nt(dm, v)
        dv_ref[:, part] = tn(probs.astype(BF16), dm).astype(BF16)
        d_scores = probs * (d_probs - jnp.sum(d_probs * probs, -1, keepdims=True))
        d_scores = d_scores.astype(BF16)
        dq_ref[:, part] = (nn(d_scores, k) * HD**-0.5).astype(BF16)
        dk_ref[:, part] = (tn(d_scores, q) * HD**-0.5).astype(BF16)
    scale_one = inv_rms(x)
    normed = (x * scale_one * gain_one[...]).astype(BF16)
    grads[0] = tn(dq_ref[...], normed).astype(BF16)
    grads[1] = tn(dk_ref[...], normed).astype(BF16)
    grads[2] = tn(dv_ref[...], normed).astype(BF16)
    d_normed = nn(dq_ref[...], table[0]) + nn(dk_ref[...], table[1]) + nn(dv_ref[...], table[2])
    grad_gain_one = jnp.sum(d_normed * x * scale_one, 0, keepdims=True)
    weighted = d_normed * gain_one[...]
    d_first = weighted * scale_one - x * (
        scale_one * scale_one * scale_one * jnp.mean(weighted * x, -1, keepdims=True)
    )
    delta = attended + jnp.sum(branch_ref[...].astype(F32), 0)
    updated_ref[...] = (x + gate * delta).astype(BF16)
    d_gate = jnp.sum(chosen_grad * delta, -1, keepdims=True)
    chosen_ref[...] = (chosen_grad + d_middle + d_first + d_gate * router[...]).astype(BF16)
    room = out_ref.shape[1] // 2
    for t in range(tensor_size):
        rows = run_rows(start_ref[t], count, room)
        out_ref[t, :room] = tn(rows, updated_ref[...]).astype(BF16)
        out_ref[t, room:] = tn(rows, chosen_ref[...]).astype(BF16)
    grad_router = jnp.sum(d_gate * x, 0, keepdims=True)
    small_ref[...] = jnp.concatenate(
        [grad_router, grad_gain_one, grad_gain_two, jnp.zeros((EXTRA - 3, model), F32)], 0
    ).astype(BF16)
    for which, out in ((core, keep_ref), (1 - core, send_ref)):
        for c in range(pieces):
            for z in range(tensor_size):
                for t in range(types):
                    for h in range(per_shard):
                        source = (z * per_shard + h) * HD + c * width
                        start = ((z * types + t) * per_shard + h) * width
                        out[c, start : start + width, :] = grads[
                            2 * which + t, source : source + width, :
                        ]


def hidden_finish_kernel(pieces, place_ref, *refs):
    up_ref, down_ref, up_rows = refs[2 * pieces :]
    chip, core = place_ref[0], place_ref[1]
    width = refs[0].shape[0] // 2
    for side in range(2):
        for k in range(pieces):
            piece = refs[side * pieces + k]
            source = 2 * (chip ^ k) + (core ^ side)
            rows = pl.ds(pl.multiple_of(source * width, width), width)
            up_rows[rows, :] = piece[:width, :]
            down_ref[rows, :] = piece[width:, :].astype(F32)
    up_ref[...] = up_rows[...].T.astype(F32)


def attn_finish_kernel(pieces, place_ref, *refs):
    query_ref, key_ref, value_ref, out_ref, table = refs[2 * pieces :]
    chip, core = place_ref[0], place_ref[1]
    heads = query_ref.shape[0] // HD
    width = HD // pieces
    for side in range(2):
        for k in range(pieces):
            piece = refs[side * pieces + k]
            for t in range(2):
                for h in range(heads):
                    start = (t * heads + h) * width
                    rows = pl.ds(pl.multiple_of(h * HD + (chip ^ k) * width, width), width)
                    table[2 * (core ^ side) + t, rows, :] = piece[
                        start : start + width, :
                    ].astype(F32)
    for t, ref in enumerate((query_ref, key_ref, value_ref, out_ref)):
        ref[...] = table[t]


def join_kernel(*refs):
    start = 0
    for ref in refs[:-1]:
        rows = ref.shape[0]
        refs[-1][start : start + rows, :] = ref[...]
        start += rows


def flag_kernel(*refs):
    top = refs[0][...].astype(F32)
    for ref in refs[1:-1]:
        top = jnp.maximum(top, ref[...].astype(F32))
    refs[-1][0] = jnp.max(top)


FREE = pl.CostEstimate(flops=1, bytes_accessed=1, transcendentals=0)


def call(kernel, outs, args, scratch=(), limit=16 * MIB):
    whole = pl.BlockSpec(memory_space=pltpu.VMEM)
    in_specs = [
        pl.BlockSpec(memory_space=pltpu.SMEM) if a.ndim == 1 else whole for a in args
    ]
    return pl.pallas_call(
        kernel,
        out_shape=outs,
        in_specs=in_specs,
        out_specs=[whole] * len(outs),
        scratch_shapes=scratch,
        compiler_params=pltpu.CompilerParams(vmem_limit_bytes=limit),
        cost_estimate=FREE,
    )(*args)


def join(*parts):
    rows = sum(p.shape[0] for p in parts)
    shape = jax.ShapeDtypeStruct((rows, parts[0].shape[1]), parts[0].dtype)
    return call(join_kernel, [shape], list(parts))[0]


def local(
    dp_size,
    tensor_size,
    tokens,
    segment_ids,
    selected,
    w_router,
    gain_one,
    w_query,
    w_key,
    w_value,
    w_out,
    gain_two,
    w_up,
    w_down,
    grad_out,
):
    row_count, local_len, model = tokens.shape
    picks = selected.shape[1]
    full_len = segment_ids.shape[1]
    width = HD // CHIPS
    per_shard = w_query.shape[1] // HD
    hidden_count = w_up.shape[1]
    hidden_width = hidden_count // GROUP
    assert row_count == tensor_size and dp_size % GROUP == 0
    dp_index = lax.axis_index(DP)
    my_z = lax.axis_index("tensor")
    member = dp_index % GROUP
    core, chip = member % 2, member // 2
    tie = lax.optimization_barrier

    def to_peer(values, step):
        return lax.ppermute(values, DP, [(i, i ^ step) for i in range(dp_size)])

    def to_core(values):
        return to_peer(values, 1)

    def to_chip(values, k):
        return to_peer(values, 2 * k)

    def to_z(values, k):
        return lax.ppermute(values, "tensor", [(i, i ^ k) for i in range(tensor_size)])

    def over_z(values):
        return [values] + [to_z(values, k) for k in range(1, tensor_size)]

    def over_chips(values):
        return [values] + [to_chip(values, k) for k in range(1, CHIPS)]

    def over_group(values):
        own = over_chips(values)
        return own + [to_core(v) for v in own]

    def row_of(values, k):
        return lax.dynamic_index_in_dim(values, my_z ^ k, 0, keepdims=False)

    def trade_z(parts):
        return [parts[0]] + [to_z(parts[k], k) for k in range(1, tensor_size)]

    def trade_shards(parts):
        stack = jnp.stack(parts)
        return trade_z([row_of(stack, k) for k in range(tensor_size)])

    def trade_chips(parts):
        return [parts[0]] + [to_chip(parts[k], k) for k in range(1, CHIPS)]

    def all_z(values):
        return lax.all_to_all(values, "tensor", 0, 0, tiled=True)

    def shape(*dims, dtype=BF16):
        return jax.ShapeDtypeStruct(dims, dtype)

    def summed(parts):
        return call(sum_kernel, [shape(*parts[0].shape)], parts)[0]

    def over_groups(values):
        step = GROUP
        while step < dp_size:
            values = summed([values, to_peer(values, step)])
            step *= 2
        return values

    row_bf, row_f32 = shape(picks, model), shape(picks, model, dtype=F32)

    def chip_rows(values):
        values = values.reshape(per_shard, CHIPS, width, model)
        return lax.dynamic_index_in_dim(values, chip, 1, keepdims=False)

    first = jnp.where(core == 0, chip_rows(w_query.T), chip_rows(w_value.T))
    second = jnp.where(core == 0, chip_rows(w_key.T), chip_rows(w_out))
    attn_mine = jnp.stack([first, second]).reshape(2 * per_shard * width, model)
    attn_parts = over_z(attn_mine)
    up_mine = lax.dynamic_slice_in_dim(w_up, member * hidden_width, hidden_width, 1)
    down_mine = lax.dynamic_slice_in_dim(w_down, member * hidden_width, hidden_width, 0)
    up_mine, down_mine = tie((up_mine, down_mine))
    ffn_mine = jnp.concatenate([up_mine.T, down_mine], 0)

    room = 3 * picks // (2 * tensor_size)
    local_start = my_z * local_len
    order = jnp.arange(picks, dtype=jnp.int32)
    slot = jnp.arange(room, dtype=jnp.int32)
    edges = jnp.arange(tensor_size + 1, dtype=jnp.int32) * local_len
    counts = jnp.sum((selected[:, None, :] < edges[None, :, None]).astype(jnp.int32), -1)
    most = jnp.max(counts[:, 1:] - counts[:, :-1]).astype(BF16)
    run_start = jnp.sum((selected < local_start).astype(jnp.int32), 1)
    window = order[None, None, :] == run_start[:, None, None] + slot[None, :, None]
    picked = jnp.sum(jnp.where(window, selected[:, None, :] + 1, 0), -1) - 1
    my_sel = lax.dynamic_index_in_dim(selected, my_z, 0, keepdims=False)
    my_seg = lax.dynamic_index_in_dim(segment_ids, my_z, 0, keepdims=False)
    start_all = jnp.sum((my_sel[None, :] < edges[:-1, None]).astype(jnp.int32), -1)
    full_pos = jnp.arange(full_len, dtype=jnp.int32)
    tags = jnp.sum(jnp.where(my_sel[:, None] == full_pos[None, :], my_seg[None, :], 0), 1)
    tag_col, tag_row = tags[:, None], tags[None, :]
    core_arr = core.reshape(1)
    g_one, g_two = gain_one[None, :], gain_two[None, :]
    router = w_router.astype(F32)[None, :]

    runs = pl.pallas_call(
        take_kernel,
        out_shape=shape(row_count, 2 * room, model),
        grid=(row_count,),
        in_specs=[
            pl.BlockSpec(memory_space=pltpu.SMEM),
            pl.BlockSpec((1, room, 1), lambda r: (r, 0, 0)),
            pl.BlockSpec((1, local_len, model), lambda r: (r, 0, 0)),
            pl.BlockSpec((1, local_len, model), lambda r: (r, 0, 0)),
        ],
        out_specs=pl.BlockSpec((1, 2 * room, model), lambda r: (r, 0, 0)),
        compiler_params=pltpu.CompilerParams(vmem_limit_bytes=16 * MIB),
        cost_estimate=FREE,
    )(local_start.reshape(1), picked[:, :, None], tokens, grad_out)
    ffn_all = jnp.broadcast_to(ffn_mine[None], (tensor_size, *ffn_mine.shape))
    small_inputs = (tag_col, tag_row, g_one, g_two, router, start_all, ffn_all)
    runs, attn_parts, small_inputs = tie((runs, attn_parts, small_inputs))
    tag_col, tag_row, g_one, g_two, router, start_all, ffn_all = small_inputs
    runs = all_z(runs)

    flag = jnp.full((EXTRA, model), most, BF16)
    half, part = tensor_size // 2, attn_mine.shape[0]
    first, second = join(*attn_parts[:half], flag), join(*attn_parts[half:])
    first = join(first, to_chip(first, 1))
    second = join(second, to_chip(second, 2))
    attn_own = [first, second, to_chip(first, 2), to_chip(second, 1)]
    places = [[None] * tensor_size for _ in range(CHIPS)]
    for c in range(CHIPS):
        for z in range(half):
            places[c][z] = (2 * (c // 2), (c % 2) * (half * part + EXTRA) + z * part)
            places[c][half + z] = (1 + 2 * (c % 2), (c // 2) * half * part + z * part)
    attn_oth = [to_core(piece) for piece in attn_own]
    attn_own, attn_oth = tie((attn_own, attn_oth))
    flags = [(i, row) for i in (0, 2) for row in (half * part, 2 * half * part + EXTRA)]
    most = pl.pallas_call(
        flag_kernel,
        out_shape=jax.ShapeDtypeStruct((1,), F32),
        grid=(1,),
        in_specs=[
            pl.BlockSpec((EXTRA, 128), lambda i, at=row // EXTRA: (at, 0)) for _, row in flags
        ]
        * 2,
        out_specs=pl.BlockSpec(memory_space=pltpu.SMEM),
        cost_estimate=FREE,
    )(*[side[i] for side in (attn_own, attn_oth) for i, _ in flags])
    step = GROUP
    while step < dp_size:
        most = jnp.maximum(most, to_peer(most, step))
        step *= 2
    crowded = most[0] > room


    local_pos = local_start + jnp.arange(local_len, dtype=jnp.int32)

    def dense_hit():
        return (selected[:, :, None] == local_pos[None, None, :]).astype(BF16)

    def take_dense(values):
        whole = jnp.einsum("rkl,rld->rkd", dense_hit(), values, preferred_element_type=F32)
        whole = whole.astype(BF16)
        return sum(trade_z([row_of(whole, k) for k in range(tensor_size)]))

    def gather_dense():
        chosen, grads = take_dense(tokens), take_dense(grad_out)
        scaled = gate_of(chosen.astype(F32), router) * grads.astype(F32)
        return [jnp.concatenate([chosen, grads], 0), scaled.astype(BF16)]

    pair, d_branch = lax.cond(
        crowded,
        gather_dense,
        lambda: list(
            call(gather_kernel, [shape(2 * picks, model), row_bf], [start_all, router, runs])
        ),
    )
    ffn_all, pair, d_branch = tie((ffn_all, pair, d_branch))
    d_branch_all = over_chips(d_branch)
    ffn_z = all_z(ffn_all)

    heads = per_shard * tensor_size
    head_dims = heads * HD
    table = pltpu.VMEM((4, head_dims, model), BF16)
    weights = attn_own + attn_oth
    q, k, v, mixed, lse, attended, normed_two = call(
        functools.partial(attend_kernel, tensor_size, places, len(attn_own)),
        [row_bf] * 4 + [shape(picks, heads, dtype=F32), row_f32, row_bf],
        [core_arr, pair, tag_col, tag_row, g_one, g_two] + weights,
        [table],
        limit=61 * MIB,
    )
    normed_two, d_branch_all = tie((normed_two, d_branch_all))
    d_branch_all = d_branch_all + [to_core(v) for v in d_branch_all]
    normed_two_all = over_group(normed_two)

    block = shape(CHIPS, picks, model)
    pre, br_keep, br_send = call(
        functools.partial(hidden_kernel, GROUP),
        [shape(CHIPS, 2 * picks, tensor_size * hidden_width, dtype=F32), block, block],
        normed_two_all + [ffn_z],
        limit=61 * MIB,
    )
    chip_arr = chip.reshape(1)
    branches = call(add_stack_kernel, [block], [chip_arr, br_keep, to_core(br_send)])[0]
    branches = lax.all_to_all(branches, "chip", 0, 0, tiled=True)
    results = call(
        functools.partial(hidden_back_kernel, GROUP),
        [shape(*ffn_mine.shape)] * tensor_size + [block] + [row_bf] * CHIPS,
        normed_two_all + d_branch_all + [ffn_z, pre],
        limit=61 * MIB,
    )
    ffn_grads, dn_keep, dn_send = results[:tensor_size], results[tensor_size], results[-CHIPS:]
    outs = [row_f32] + [row_bf] * (CHIPS - 1)
    d_norms = call(add_kernel, outs, [dn_keep] + [to_core(v) for v in dn_send])
    d_norms = trade_chips(list(d_norms))
    ffn_grads = trade_shards(ffn_grads)
    d_norms, ffn_grads[1], ffn_grads[2] = tie((d_norms, ffn_grads[1], ffn_grads[2]))

    body = tensor_size * 2 * per_shard * width
    packed = shape(CHIPS, body, model)
    keep, give, small, out_runs, updated, d_chosen = call(
        functools.partial(back_kernel, tensor_size, places, len(attn_own)),
        [packed, packed, shape(EXTRA, model), shape(tensor_size, 2 * room, model)]
        + [row_bf, row_bf],
        [core_arr, start_all, pair, attended, q, k, v, mixed, lse]
        + [tag_col, tag_row, g_one, g_two, router]
        + weights
        + d_norms
        + [branches],
        [table, table] + [pltpu.VMEM((picks, head_dims), BF16)] * 3,
        limit=61 * MIB,
    )
    halves = call(
        halves_kernel,
        [shape(body + EXTRA, model)] * CHIPS,
        [keep, to_core(give), small, to_core(small)],
    )
    attn_recv = trade_chips(list(halves))
    attn_recv, ffn_grads[3] = tie((attn_recv, ffn_grads[3]))
    out_runs = all_z(out_runs)

    ffn_sum = over_groups(summed(ffn_grads))
    place_arr = jnp.stack([chip, core])
    shards = call(
        functools.partial(shards_kernel, CHIPS),
        [shape(part + EXTRA, model)] * tensor_size,
        attn_recv,
    )
    shards, ffn_sum, out_runs = tie((shards, ffn_sum, out_runs))
    ffn_last = over_group(ffn_sum)
    square = shape(hidden_count, model, dtype=F32)
    grad_up, grad_down = call(
        functools.partial(hidden_finish_kernel, CHIPS),
        [shape(model, hidden_count, dtype=F32), square],
        [place_arr] + ffn_last,
        [pltpu.VMEM(square.shape, BF16)],
    )
    z_recv = trade_z(shards)

    def place(hits, values, initial):
        covered = jnp.any(hits > 0, axis=1)[:, :, None]
        placed = jnp.einsum("rkl,rkd->rld", hits, values, preferred_element_type=F32)
        return jnp.where(covered, placed.astype(BF16), initial)

    def place_dense(values, initial):
        parts = [lax.all_gather(v, "tensor", axis=0) for v in jnp.split(values, 2, 0)]
        return place(dense_hit(), jnp.concatenate(parts, 1), initial)

    def place_runs():
        run_hit = (picked[:, :, None] == local_pos[None, None, :]).astype(BF16)
        return (
            place(run_hit, out_runs[:, :room], tokens),
            place(run_hit, out_runs[:, room:], grad_out),
        )

    layer_out, grad_tokens = lax.cond(
        crowded,
        lambda: (place_dense(updated, tokens), place_dense(d_chosen, grad_out)),
        place_runs,
    )

    z_recv, layer_out, grad_tokens = tie((z_recv, layer_out, grad_tokens))
    attn_sum = over_groups(summed(z_recv))

    small = attn_sum[part:].astype(F32)
    table_shape = (4, per_shard * HD, model)
    attn_all = call(
        functools.partial(attn_finish_kernel, CHIPS),
        [shape(*table_shape[1:], dtype=F32)] * 4,
        [place_arr] + over_group(attn_sum[:part]),
        [pltpu.VMEM(table_shape, F32)],
    )
    return (
        layer_out,
        grad_tokens,
        small[0],
        small[1],
        attn_all[0].T,
        attn_all[1].T,
        attn_all[2].T,
        attn_all[3],
        small[2],
        grad_up,
        grad_down,
    )


def solution(mesh):
    groups, tensor_size = mesh.shape["dp"] // GROUP, mesh.shape["tensor"]
    split = jax.sharding.Mesh(
        mesh.devices.reshape(groups, CHIPS, 2, tensor_size), (*DP, "tensor")
    )
    tokens, picks = P(DP, "tensor", None), P(DP, None)
    columns, rows = P(None, "tensor"), P("tensor", None)
    weights = (columns, columns, columns, rows, P(), columns, rows)
    return jax.shard_map(
        functools.partial(local, mesh.shape["dp"], tensor_size),
        mesh=split,
        in_specs=(tokens, picks, picks, P(), P(), *weights, tokens),
        out_specs=(tokens, tokens, P(), P(), *weights),
        check_vma=False,
    )
```
